32 devices in a mesh: groups: 2 (over y), row: 4 (over z), col: 4 (over x, core).
Axes of the slice: x: 2, y: 2, z: 4, core: 2. Of those that a mesh axis runs over, the one named last changes fastest.
Arguments:
- a_blocks: bfloat16 [8, 4, 16, 128, 128], P(('groups', 'row'), 'col'), parts along dimension 0, may hold values from -0.5 to 0.5
- a_index: int32 [8, 4, 2, 16], P(('groups', 'row'), 'col'), parts along dimension 0, may hold values from 0 to 7, as said below
- a_live: int32 [8, 4], P(('groups', 'row'), 'col'), parts along dimension 0, may hold values from 4 to 16, as said below
- b_blocks: bfloat16 [8, 4, 1, 3, 128, 128], P(('groups', 'row'), 'col'), parts along dimension 0, may hold values from -6 to 6
- b_index: int32 [8, 4, 1, 2, 3], P(('groups', 'row'), 'col'), parts along dimension 0, may hold values from 0 to 7, as said below
- c_keep: int32 [32, 8], P(('groups', 'col'), 'row'), parts along dimension 0, may hold values 0 or 1
Outputs:
- c_out: bfloat16 [4096, 1024], P(('groups', 'col'), 'row'), parts along dimension 0
The draws below stay inside these ranges and needn't reach their ends.
There are 2 independent parts, one for each index of `groups`. The reference program is written for one: setup_inputs(seed, part) draws one part's arguments, and reference() takes and returns one part's arrays. A program takes and returns all parts, laid end to end along the dimension named above; each array names one. Nothing has to cross between parts.
Inputs may be any that keep to these rules, and one draw needn't show every extreme that they name: `a_index`: within one panel the pairs (block row, inner block) are distinct; block rows are below 4, inner blocks below 8. `a_live`: some panel holds all 16 slots in every draw. `b_index`: within one panel the pairs (inner block, block column) are distinct; inner blocks are below 8, block columns below 2.
All inputs are finite; a program needn't handle non-finite values. No bound on the sum of `c_keep` on one device may be relied on, other than what follows from the above.
Results may differ from the reference program's by a relative error of at most 0.001.
Values may be sent and summed in bfloat16 or wider, within the bound.
A program may use at most 64 MiB of HBM per device.

```python
import jax
import jax.numpy as jnp
from jax import lax

BS = 128
MR = 4
NC = 2
KP = 8
NZA = 16
NZB = 3
KPAN = 4
RGRP = 4
CGRP = 4
BCOL = 4
MB = 1
KEEPR = 16
KEEPC = 8
CROWS = 2048
CCOLS = 1024


def draw_a_index(key, part):
    key = jax.random.fold_in(key, 11)
    keys = jax.random.split(key, KPAN * RGRP)
    slot_ids = jax.vmap(lambda one_key: jax.random.permutation(one_key, MR * KP)[:NZA])(keys)
    stacked = jnp.stack([slot_ids // KP, slot_ids % KP], axis=1)
    return stacked.reshape(KPAN, RGRP, 2, NZA).astype(jnp.int32)


def draw_a_live(key, part):
    key = jax.random.fold_in(key, 12)
    count_key, pick_key = jax.random.split(key)
    counts = jax.random.randint(count_key, (KPAN * RGRP,), max(1, NZA // 4), NZA + 1)
    chosen = jax.random.randint(pick_key, (), 0, KPAN * RGRP)
    counts = counts.at[chosen].set(NZA)
    return counts.reshape(KPAN, RGRP).astype(jnp.int32)


def draw_b_index(key, part):
    key = jax.random.fold_in(key, 13)
    keys = jax.random.split(key, CGRP * BCOL * MB)
    slot_ids = jax.vmap(lambda one_key: jax.random.permutation(one_key, KP * NC)[:NZB])(keys)
    stacked = jnp.stack([slot_ids // NC, slot_ids % NC], axis=1)
    return stacked.reshape(CGRP, BCOL, MB, 2, NZB).astype(jnp.int32)


def with_ends(entries, own_key, low, high):
    shape = entries.shape
    place = [jax.random.randint(jax.random.fold_in(own_key, axis), (), 0, shape[axis]) for axis in range(len(shape))]
    entries = entries.at[tuple(place)].set(low)
    longest = shape.index(max(shape))
    place[longest] = (place[longest] + 1) % shape[longest]
    return entries.at[tuple(place)].set(high)


def block_scale(stream_key, shape, pieces, least, high):
    def one(axis_at, shards_of):
        heights = jax.random.uniform(jax.random.fold_in(jax.random.fold_in(stream_key, 6), axis_at), (shards_of,), jnp.float32, least / len(pieces), high / len(pieces))
        return jnp.repeat(jnp.exp(heights), shape[axis_at] // shards_of).reshape((-1,) + (1,) * (len(shape) - axis_at - 1))

    gain = one(*pieces[0])
    for cut in pieces[1:]:
        gain = gain * one(*cut)
    return gain


def bell_draw(stream_key, dims, deviation, most, pieces=(), held_as=jnp.bfloat16):
    result = jax.random.normal(stream_key, dims, jnp.float32) * deviation
    if len(pieces) > 0:
        result = block_scale(stream_key, dims, pieces, -0.22, 0.18) * result
    return jnp.clip(result, min=-most, max=most).astype(held_as)


def setup_inputs(seed: int = 0, part: int = 0) -> dict:
    streams_of = jax.random.split(jax.random.key(seed), 7)
    part_keys = jax.random.split(jax.random.fold_in(streams_of[6], part), 7)
    a_blocks = bell_draw(part_keys[0], (KPAN, RGRP, NZA, BS, BS), BS ** -0.5, 0.5, ((0, 4), (1, 4)))
    a_index = draw_a_index(jax.random.fold_in(jax.random.fold_in(streams_of[6], part), 71), part)
    a_live = draw_a_live(jax.random.fold_in(jax.random.fold_in(streams_of[6], part), 71), part)
    b_blocks = bell_draw(part_keys[3], (CGRP, BCOL, MB, NZB, BS, BS), 1.0, 6.0, ((0, 4), (1, 4)))
    b_index = draw_b_index(jax.random.fold_in(jax.random.fold_in(streams_of[6], part), 71), part)
    c_keep = with_ends((jax.random.randint(part_keys[5], (KEEPR, KEEPC), 0, 4) < 3).astype(jnp.int32), jax.random.fold_in(part_keys[5], 1), 0, 1)
    return {"a_blocks": a_blocks, "a_index": a_index, "a_live": a_live, "b_blocks": b_blocks, "b_index": b_index, "c_keep": c_keep}


def panel_product(first_blocks, first_index, first_live, second_blocks, second_index):
    slot_ids = second_index[0] * NC + second_index[1]
    slot_range = jnp.arange(KP * NC, dtype=jnp.int32)
    picker = (slot_range[:, None] == slot_ids[None, :]).astype(jnp.float32).reshape(KP, NC, NZB)
    dense_b = jnp.einsum("kcz,zuv->kucv", picker, second_blocks.astype(jnp.float32), precision=lax.Precision.HIGHEST)
    dense_b = dense_b.astype(jnp.bfloat16).reshape(KP, BS, NC * BS)
    chosen = jnp.take(dense_b, first_index[1].astype(jnp.int32), axis=0)
    live_mask = (jnp.arange(NZA, dtype=jnp.int32) < first_live).astype(jnp.float32)
    products = jnp.einsum("zuv,zvw->zuw", first_blocks.astype(jnp.float32), chosen.astype(jnp.float32), precision=lax.Precision.HIGHEST)
    products = products * live_mask[:, None, None]
    row_hot = (jnp.arange(MR, dtype=jnp.int32)[:, None] == first_index[0][None, :]).astype(jnp.float32)
    return jnp.einsum("rz,zuw->ruw", row_hot, products, precision=lax.Precision.HIGHEST)


def reference(a_blocks, a_index, a_live, b_blocks, b_index, c_keep):
    tick_total = min(6, KPAN)

    def one_group(group_id):
        def one_column(column_id):
            total = jnp.zeros((MR, BS, NC * BS), jnp.float32)
            for tick_no in range(tick_total):
                panel_id = ((group_id + column_id + tick_no) % KPAN).astype(jnp.int32)
                owner_id = (panel_id % BCOL).astype(jnp.int32)
                depth_id = (panel_id // BCOL).astype(jnp.int32)
                total = total + panel_product(a_blocks[panel_id, group_id], a_index[panel_id, group_id], a_live[panel_id, group_id], b_blocks[column_id, owner_id, depth_id], b_index[column_id, owner_id, depth_id])
            return total
        return jax.vmap(one_column)(jnp.arange(CGRP, dtype=jnp.int32))

    grouped = lax.map(one_group, jnp.arange(RGRP, dtype=jnp.int32))
    grouped = grouped.reshape(RGRP, CGRP, MR, BS, NC, BS).transpose(0, 2, 3, 1, 4, 5)
    keep_mask = c_keep.reshape(RGRP, MR, CGRP, NC).astype(jnp.float32)
    grouped = grouped * keep_mask[:, :, None, :, :, None]
    return grouped.reshape(CROWS, CCOLS).astype(jnp.bfloat16)
```

```python
import jax
import jax.numpy as jnp
from jax import lax
from jax.experimental import pallas as pl
from jax.experimental.pallas import tpu as pltpu
from jax.sharding import PartitionSpec as P

BS = 128
MR = 4
NC = 2
KP = 8
NZA = 16
NZB = 3


def as_sent(array):
    return jax.tree.map(lambda a: a.astype(jnp.bfloat16) if a.dtype == jnp.float32 else a, array)


def passed_along(value, axis, steps):
    count = lax.axis_size(axis)
    pairs = [(source, (source + steps) % count) for source in range(count)]
    return lax.ppermute(value, axis, pairs)


def panel_product(total, first_blocks, first_index, first_live, second_blocks, second_index):
    slot_ids = second_index[0] * NC + second_index[1]
    slot_range = jnp.arange(KP * NC, dtype=jnp.int32)
    picker = (slot_range[:, None] == slot_ids[None, :]).astype(jnp.bfloat16).reshape(KP, NC, NZB)
    dense_b = jnp.einsum(
        "kcz,zuv->kucv", picker, second_blocks, preferred_element_type=jnp.bfloat16
    )
    dense_b = dense_b.reshape(KP * BS, NC * BS)
    live_mask = (jnp.arange(NZA, dtype=jnp.int32) < first_live).astype(jnp.bfloat16)
    row_hot = (jnp.arange(MR, dtype=jnp.int32)[:, None] == first_index[0][None, :]).astype(
        jnp.bfloat16
    )
    inner_hot = (jnp.arange(KP, dtype=jnp.int32)[:, None] == first_index[1][None, :]).astype(
        jnp.bfloat16
    )
    placer = row_hot[:, None, :] * inner_hot[None, :, :] * live_mask[None, None, :]
    dense_a = jnp.einsum("rkz,zuv->rukv", placer, first_blocks, preferred_element_type=jnp.bfloat16)
    dense_a = dense_a.reshape(MR * BS, KP * BS)
    return total + jnp.dot(dense_a, dense_b, preferred_element_type=jnp.float32)


def local(a_blocks, a_index, a_live, b_blocks, b_index, c_keep):
    row_count = lax.axis_size("row")
    col_count = lax.axis_size("col")
    row_pos = lax.axis_index("row")
    col_pos = lax.axis_index("col")
    tick_total = min(6, row_count)
    bit_total = col_count.bit_length() - 1
    a_state = (a_blocks, a_index, a_live)
    for bit_pos in range(bit_total):
        shifted = jax.tree.map(
            lambda part, own: part.astype(own.dtype),
            passed_along(as_sent(a_state), "row", -(1 << bit_pos)),
            a_state,
        )
        take_bit = col_pos // (1 << bit_pos) % 2 == 1
        a_state = jax.tree.map(
            lambda incoming, current: jnp.where(take_bit, incoming, current), shifted, a_state
        )
    skew_amount = row_pos % col_count
    b_state = (b_blocks, b_index)
    for bit_pos in range(bit_total):
        shifted = jax.tree.map(
            lambda part, own: part.astype(own.dtype),
            passed_along(as_sent(b_state), "col", -(1 << bit_pos)),
            b_state,
        )
        take_bit = skew_amount // (1 << bit_pos) % 2 == 1
        b_state = jax.tree.map(
            lambda incoming, current: jnp.where(take_bit, incoming, current), shifted, b_state
        )
    total = jnp.zeros((MR * BS, NC * BS), jnp.float32)
    for tick_no in range(tick_total):
        panel_id = (col_pos + row_pos + tick_no) % row_count
        depth_id = panel_id // col_count
        group_blocks = b_state[0][0, 0]
        group_index = b_state[1][0, 0]
        second_blocks = lax.dynamic_index_in_dim(group_blocks, depth_id, 0, keepdims=False)
        second_index = lax.dynamic_index_in_dim(group_index, depth_id, 0, keepdims=False)
        first_blocks, first_index, first_live = a_state
        total = panel_product(
            total,
            first_blocks[0, 0],
            first_index[0, 0],
            first_live[0, 0],
            second_blocks,
            second_index,
        )
        if tick_no + 1 < tick_total:
            a_state = jax.tree.map(
                lambda part, own: part.astype(own.dtype),
                passed_along(as_sent(a_state), "row", -1),
                a_state,
            )
            b_state = jax.tree.map(
                lambda part, own: part.astype(own.dtype),
                passed_along(as_sent(b_state), "col", -1),
                b_state,
            )
    keep_mask = c_keep.astype(jnp.float32)
    filtered = total.reshape(MR, BS, NC, BS) * keep_mask[:, None, :, None]
    return filtered.reshape(MR * BS, NC * BS).astype(jnp.bfloat16)


CHUNKS = (32, 32, 32, 32)
STARTS = tuple(sum(CHUNKS[:n]) for n in range(len(CHUNKS)))
NCH = len(CHUNKS)
ZERO = NZA
B_INNER = 64
B_COLUMN = 72
DEPTH = NZB * BS
WIDE = NC * BS


def line_kernel(
    a_index, a_live, b_index, c_keep, a_ref, b_ref, o_ref,
    own_a, inner_a, outer_a, far_0, far_1, far_2, far_3,
    own_b, outer_b, own_w, outer_w, own_sum, outer_sum, sum_in,
    own_tab, inner_tab, outer_tab, far_tab, own_bt, outer_bt,
    own_st, inner_st, outer_st, far_st, own_bs, outer_bs,
    local_sem, smem_sem, a_send, a_recv, tab_send, tab_recv,
    b_send, b_recv, bt_send, bt_recv, sum_send, sum_recv,
):
    far_a = (far_0, far_1, far_2, far_3)
    row = lax.axis_index("row")
    col = lax.axis_index("col")
    is_end = jnp.logical_or(row == 0, row == 3)
    is_middle = jnp.logical_not(is_end)
    outer = jnp.where(row == 1, 0, 3)
    inner = 3 - row
    beside = jnp.where(row == 0, 1, 2)
    panels = (row, inner, 3 - outer, outer)

    def to_row(src, dst, send, recv, target):
        return pltpu.make_async_remote_copy(
            src_ref=src, dst_ref=dst, send_sem=send, recv_sem=recv,
            device_id={"row": target}, device_id_type=pl.DeviceIdType.MESH,
        )

    def to_col(src, dst, send, recv, target):
        return pltpu.make_async_remote_copy(
            src_ref=src, dst_ref=dst, send_sem=send, recv_sem=recv,
            device_id={"col": target}, device_id_type=pl.DeviceIdType.MESH,
        )

    def others():
        return [lax.rem(col + step, 4) for step in range(1, 4)]

    blocks = pl.ds(0, NZA)
    copy_a = pltpu.make_async_copy(a_ref.at[0, 0], own_a.at[blocks], local_sem.at[0])
    copy_b = pltpu.make_async_copy(b_ref.at[0, 0, 0], own_b.at[col], local_sem.at[1])
    copy_a.start()
    copy_b.start()

    lane = lax.broadcasted_iota(jnp.int32, (8, BS), 1)
    table = jnp.full((8, BS), ZERO, jnp.int32)
    live = a_live[0, 0]
    for slot in range(NZA):
        place = a_index[0, 0, 0, slot] * KP + a_index[0, 0, 1, slot]
        place = jnp.where(slot < live, place, -1)
        table = jnp.where(lane == place, slot, table)
    for slot in range(NZB):
        table = jnp.where(lane == B_INNER + slot, b_index[0, 0, 0, 0, slot], table)
        table = jnp.where(lane == B_COLUMN + slot, b_index[0, 0, 0, 1, slot], table)
    own_tab[...] = table
    own_bt[col] = table
    blank = jnp.zeros((BS, BS), jnp.bfloat16)
    own_a[ZERO] = blank
    inner_a[ZERO] = blank
    outer_a[ZERO] = blank
    for n in range(NCH):
        far_a[n][ZERO] = blank[: CHUNKS[n]]

    barrier = pltpu.get_barrier_semaphore()
    for target in others():
        pl.semaphore_signal(
            barrier, inc=1, device_id={"col": target}, device_id_type=pl.DeviceIdType.MESH
        )

    @pl.when(is_end)
    def _():
        pl.semaphore_signal(
            barrier, inc=1, device_id={"row": beside}, device_id_type=pl.DeviceIdType.MESH
        )
        pl.semaphore_wait(barrier, 4)

    @pl.when(is_middle)
    def _():
        for target in (outer, inner):
            pl.semaphore_signal(
                barrier, inc=1, device_id={"row": target}, device_id_type=pl.DeviceIdType.MESH
            )
        pl.semaphore_wait(barrier, 5)

    def to_smem(src, dst, n):
        return pltpu.make_async_copy(src, dst, smem_sem.at[n])

    def place_b(w_ref, at, blocks_ref, meta, panel):
        for slot in range(NZB):
            column = meta[panel, 0, B_COLUMN + slot]
            block = blocks_ref[panel, slot].astype(jnp.float32)
            for c in range(NC):
                hot = jnp.where(column == c, 1.0, 0.0)
                w_ref[pl.ds(at * DEPTH + slot * BS, BS), pl.ds(c * BS, BS)] = (
                    block * hot
                ).astype(jnp.bfloat16)

    def picked(a_buf, tab, meta, panel, r):
        return jnp.concatenate(
            [a_buf[tab[0, r * KP + meta[panel, 0, B_INNER + slot]]] for slot in range(NZB)],
            axis=1,
        )

    def times(x, w_ref, at):
        return jnp.dot(
            x, w_ref[pl.ds(at * DEPTH, DEPTH), :], preferred_element_type=jnp.float32
        )

    def store(r, start, size, value):
        for c in range(NC):
            kept = value[:, c * BS : (c + 1) * BS] * c_keep[r, c].astype(jnp.float32)
            o_ref[pl.ds(r * BS + start, size), pl.ds(c * BS, BS)] = kept.astype(jnp.bfloat16)

    @pl.when(is_end)
    def _():
        sends = [
            to_row(own_tab, outer_tab, tab_send.at[0], tab_recv.at[0], beside),
            to_row(own_bt.at[col], outer_bt.at[col], tab_send.at[1], bt_recv.at[1, col], beside),
            to_row(b_ref.at[0, 0, 0], outer_b.at[col], b_send.at[0, 0], b_recv.at[1, col], beside),
        ]
        for n in range(NCH):
            piece = pl.ds(STARTS[n], CHUNKS[n])
            sends.append(
                to_row(
                    a_ref.at[0, 0, :, piece, :], outer_a.at[blocks, piece, :],
                    a_send.at[n], a_recv.at[n], beside,
                )
            )
        for send in sends:
            send.start()

        def shared():
            out = []
            for n, target in enumerate(others()):
                out.append(
                    to_col(b_ref.at[0, 0, 0], own_b.at[col], b_send.at[1, n], b_recv.at[0, col], target)
                )
                out.append(
                    to_col(own_tab, own_bt.at[col], bt_send.at[0, n], bt_recv.at[0, col], target)
                )
            return out

        @pl.when(col == row)
        def _():
            for send in shared():
                send.start()

        @pl.when(col != row)
        def _():
            to_col(own_bt.at[row], own_bt.at[row], bt_send.at[0, 0], bt_recv.at[0, row], col).wait_recv()
            to_col(own_b.at[row], own_b.at[row], b_send.at[1, 0], b_recv.at[0, row], col).wait_recv()

        loads = [to_smem(own_tab, own_st, 0), to_smem(own_bt, own_bs, 1)]
        for load in loads:
            load.start()
        copy_a.wait()
        copy_b.wait()
        for load in loads:
            load.wait()
        place_b(own_w, 0, own_b, own_bs, row)

        def own_part(r, carry):
            own_sum[r] = times(picked(own_a, own_st, own_bs, row, r), own_w, 0)
            return carry

        lax.fori_loop(0, MR, own_part, 0)
        for n in range(NCH):
            piece = pl.ds(STARTS[n], CHUNKS[n])
            to_row(
                sum_in.at[:, piece, :], sum_in.at[:, piece, :],
                sum_send.at[n], sum_recv.at[n], beside,
            ).wait_recv()
            for r in range(MR):
                store(r, STARTS[n], CHUNKS[n], own_sum[r, piece, :] + sum_in[r, piece, :])
        for send in sends:
            send.wait_send()

        @pl.when(col == row)
        def _():
            for send in shared():
                send.wait_send()

    @pl.when(is_middle)
    def _():
        sends = [
            to_row(own_tab, inner_tab, tab_send.at[0], tab_recv.at[1], inner),
            to_row(a_ref.at[0, 0], inner_a.at[blocks], a_send.at[NCH], a_recv.at[NCH], inner),
        ]
        for n, target in enumerate(others()):
            sends.append(
                to_col(own_tab, own_bt.at[col], bt_send.at[0, n], bt_recv.at[0, col], target)
            )
            sends.append(
                to_col(b_ref.at[0, 0, 0], own_b.at[col], b_send.at[0, n], b_recv.at[0, col], target)
            )
        for send in sends:
            send.start()

        to_row(outer_tab, outer_tab, tab_send.at[1], tab_recv.at[0], outer).wait_recv()
        onward = [to_row(outer_tab, far_tab, tab_send.at[1], tab_recv.at[2], inner)]
        onward[0].start()

        def passed_b():
            out = []
            for n, target in enumerate(others()):
                out.append(
                    to_col(outer_bt.at[col], outer_bt.at[col], bt_send.at[1, n], bt_recv.at[1, col], target)
                )
                out.append(
                    to_col(outer_b.at[col], outer_b.at[col], b_send.at[1, n], b_recv.at[1, col], target)
                )
            return out

        to_row(outer_bt.at[col], outer_bt.at[col], tab_send.at[1], bt_recv.at[1, col], outer).wait_recv()
        to_row(outer_b.at[col], outer_b.at[col], tab_send.at[1], b_recv.at[1, col], outer).wait_recv()

        @pl.when(col != outer)
        def _():
            for send in passed_b():
                send.start()

        for n in range(NCH):
            piece = pl.ds(STARTS[n], CHUNKS[n])
            part = outer_a.at[blocks, piece, :]
            to_row(part, part, a_send.at[n], a_recv.at[n], outer).wait_recv()
            send = to_row(part, far_a[n].at[blocks], a_send.at[n], a_recv.at[NCH + 1 + n], inner)
            send.start()
            onward.append(send)

        for source in others():
            to_col(own_bt.at[source], own_bt.at[source], bt_send.at[0, 0], bt_recv.at[0, source], col).wait_recv()
            to_col(own_b.at[source], own_b.at[source], b_send.at[0, 0], b_recv.at[0, source], col).wait_recv()

            @pl.when(source != outer)
            def _():
                to_col(outer_bt.at[source], outer_bt.at[source], bt_send.at[0, 0], bt_recv.at[1, source], col).wait_recv()
                to_col(outer_b.at[source], outer_b.at[source], b_send.at[0, 0], b_recv.at[1, source], col).wait_recv()

        to_row(inner_tab, inner_tab, tab_send.at[1], tab_recv.at[1], inner).wait_recv()
        to_row(far_tab, far_tab, tab_send.at[1], tab_recv.at[2], inner).wait_recv()
        loads = [
            to_smem(src, dst, n)
            for n, (src, dst) in enumerate(
                (
                    (own_tab, own_st), (inner_tab, inner_st), (outer_tab, outer_st),
                    (far_tab, far_st), (own_bt, own_bs), (outer_bt, outer_bs),
                )
            )
        ]
        for load in loads:
            load.start()
        copy_a.wait()
        copy_b.wait()
        for load in loads:
            load.wait()
        for at, panel in enumerate(panels):
            place_b(own_w, at, own_b, own_bs, panel)
            if at < 3:
                place_b(outer_w, at, outer_b, outer_bs, panel)

        def own_part(r, carry):
            own_sum[r] = times(
                picked(own_a, own_st, own_bs, panels[0], r), own_w, 0
            ) + times(picked(outer_a, outer_st, own_bs, panels[3], r), own_w, 3)
            outer_sum[r] = times(picked(own_a, own_st, outer_bs, panels[0], r), outer_w, 0)
            return carry

        lax.fori_loop(0, MR, own_part, 0)
        to_row(
            inner_a.at[blocks], inner_a.at[blocks], a_send.at[0], a_recv.at[NCH], inner
        ).wait_recv()

        def inner_part(r, carry):
            own_sum[r] += times(picked(inner_a, inner_st, own_bs, panels[1], r), own_w, 1)
            outer_sum[r] += times(picked(inner_a, inner_st, outer_bs, panels[1], r), outer_w, 1)
            return carry

        lax.fori_loop(0, MR, inner_part, 0)

        def far_part(n, w_ref, meta):
            x = jnp.concatenate(
                [picked(far_a[n], far_st, meta, panels[2], r) for r in range(MR)], axis=0
            )
            return times(x, w_ref, 2).reshape(MR, CHUNKS[n], WIDE)

        for n in range(NCH):
            piece = pl.ds(STARTS[n], CHUNKS[n])
            to_row(
                far_a[n].at[blocks], far_a[n].at[blocks], a_send.at[0], a_recv.at[NCH + 1 + n], inner
            ).wait_recv()
            outer_sum[:, piece, :] += far_part(n, outer_w, outer_bs)
            send = to_row(
                outer_sum.at[:, piece, :], sum_in.at[:, piece, :],
                sum_send.at[n], sum_recv.at[n], outer,
            )
            send.start()
            onward.append(send)
            mine = own_sum[:, piece, :] + far_part(n, own_w, own_bs)
            for r in range(MR):
                store(r, STARTS[n], CHUNKS[n], mine[r])
        for send in sends + onward:
            send.wait_send()

        @pl.when(col != outer)
        def _():
            for send in passed_b():
                send.wait_send()


def line_local(a_blocks, a_index, a_live, b_blocks, b_index, c_keep):
    scalar = pl.BlockSpec(memory_space=pltpu.SMEM)
    anywhere = pl.BlockSpec(memory_space=pl.ANY)
    dma = pltpu.SemaphoreType.DMA
    panel = pltpu.VMEM((NZA + 1, BS, BS), jnp.bfloat16)
    meta = (8, BS)
    total = pltpu.VMEM((MR, BS, WIDE), jnp.float32)
    return pl.pallas_call(
        line_kernel,
        out_shape=jax.ShapeDtypeStruct((MR * BS, WIDE), jnp.bfloat16),
        in_specs=[scalar] * 4 + [anywhere] * 2,
        out_specs=pl.BlockSpec(memory_space=pltpu.VMEM),
        scratch_shapes=[panel] * 3
        + [pltpu.VMEM((NZA + 1, size, BS), jnp.bfloat16) for size in CHUNKS]
        + [pltpu.VMEM((4, NZB, BS, BS), jnp.bfloat16)] * 2
        + [pltpu.VMEM((4 * DEPTH, WIDE), jnp.bfloat16), pltpu.VMEM((3 * DEPTH, WIDE), jnp.bfloat16)]
        + [total] * 3
        + [pltpu.VMEM(meta, jnp.int32)] * 4
        + [pltpu.VMEM((4,) + meta, jnp.int32)] * 2
        + [pltpu.SMEM(meta, jnp.int32)] * 4
        + [pltpu.SMEM((4,) + meta, jnp.int32)] * 2
        + [
            dma((2,)), dma((6,)),
            dma((NCH + 1,)), dma((2 * NCH + 1,)), dma((2,)), dma((3,)),
            dma((2, 3)), dma((2, 4)), dma((2, 3)), dma((2, 4)),
            dma((NCH,)), dma((NCH,)),
        ],
        compiler_params=pltpu.CompilerParams(
            collective_id=0, has_side_effects=True, vmem_limit_bytes=32 * 1024 * 1024
        ),
    )(a_index, a_live, b_index, c_keep, a_blocks, b_blocks)


def solution(mesh):
    placed = (
        P(("groups", "row"), "col", None, None, None),
        P(("groups", "row"), "col", None, None),
        P(("groups", "row"), "col"),
        P(("groups", "row"), "col", None, None, None, None),
        P(("groups", "row"), "col", None, None, None),
        P(("groups", "col"), "row"),
    )
    short_line = mesh.shape["row"] == 4 and mesh.shape["col"] == 4
    return jax.shard_map(
        line_local if short_line else local, mesh=mesh, in_specs=placed, out_specs=P(("groups", "col"), "row"), check_vma=False
    )
```

```python
import jax
import jax.numpy as jnp
from jax import lax
from jax.experimental import pallas as pl
from jax.experimental.pallas import tpu as pltpu
from jax.sharding import PartitionSpec as P

BS = 128
MR = 4
NC = 2
KP = 8
NZA = 16
NZB = 3


def as_sent(array):
    return jax.tree.map(lambda a: a.astype(jnp.bfloat16) if a.dtype == jnp.float32 else a, array)


def passed_along(value, axis, steps):
    count = lax.axis_size(axis)
    pairs = [(source, (source + steps) % count) for source in range(count)]
    return lax.ppermute(value, axis, pairs)


def panel_product(total, first_blocks, first_index, first_live, second_blocks, second_index):
    slot_ids = second_index[0] * NC + second_index[1]
    slot_range = jnp.arange(KP * NC, dtype=jnp.int32)
    picker = (slot_range[:, None] == slot_ids[None, :]).astype(jnp.bfloat16).reshape(KP, NC, NZB)
    dense_b = jnp.einsum(
        "kcz,zuv->kucv", picker, second_blocks, preferred_element_type=jnp.bfloat16
    )
    dense_b = dense_b.reshape(KP * BS, NC * BS)
    live_mask = (jnp.arange(NZA, dtype=jnp.int32) < first_live).astype(jnp.bfloat16)
    row_hot = (jnp.arange(MR, dtype=jnp.int32)[:, None] == first_index[0][None, :]).astype(
        jnp.bfloat16
    )
    inner_hot = (jnp.arange(KP, dtype=jnp.int32)[:, None] == first_index[1][None, :]).astype(
        jnp.bfloat16
    )
    placer = row_hot[:, None, :] * inner_hot[None, :, :] * live_mask[None, None, :]
    dense_a = jnp.einsum("rkz,zuv->rukv", placer, first_blocks, preferred_element_type=jnp.bfloat16)
    dense_a = dense_a.reshape(MR * BS, KP * BS)
    return total + jnp.dot(dense_a, dense_b, preferred_element_type=jnp.float32)


def local(a_blocks, a_index, a_live, b_blocks, b_index, c_keep):
    row_count = lax.axis_size("row")
    col_count = lax.axis_size("col")
    row_pos = lax.axis_index("row")
    col_pos = lax.axis_index("col")
    tick_total = min(6, row_count)
    bit_total = col_count.bit_length() - 1
    a_state = (a_blocks, a_index, a_live)
    for bit_pos in range(bit_total):
        shifted = jax.tree.map(
            lambda part, own: part.astype(own.dtype),
            passed_along(as_sent(a_state), "row", -(1 << bit_pos)),
            a_state,
        )
        take_bit = col_pos // (1 << bit_pos) % 2 == 1
        a_state = jax.tree.map(
            lambda incoming, current: jnp.where(take_bit, incoming, current), shifted, a_state
        )
    skew_amount = row_pos % col_count
    b_state = (b_blocks, b_index)
    for bit_pos in range(bit_total):
        shifted = jax.tree.map(
            lambda part, own: part.astype(own.dtype),
            passed_along(as_sent(b_state), "col", -(1 << bit_pos)),
            b_state,
        )
        take_bit = skew_amount // (1 << bit_pos) % 2 == 1
        b_state = jax.tree.map(
            lambda incoming, current: jnp.where(take_bit, incoming, current), shifted, b_state
        )
    total = jnp.zeros((MR * BS, NC * BS), jnp.float32)
    for tick_no in range(tick_total):
        panel_id = (col_pos + row_pos + tick_no) % row_count
        depth_id = panel_id // col_count
        group_blocks = b_state[0][0, 0]
        group_index = b_state[1][0, 0]
        second_blocks = lax.dynamic_index_in_dim(group_blocks, depth_id, 0, keepdims=False)
        second_index = lax.dynamic_index_in_dim(group_index, depth_id, 0, keepdims=False)
        first_blocks, first_index, first_live = a_state
        total = panel_product(
            total,
            first_blocks[0, 0],
            first_index[0, 0],
            first_live[0, 0],
            second_blocks,
            second_index,
        )
        if tick_no + 1 < tick_total:
            a_state = jax.tree.map(
                lambda part, own: part.astype(own.dtype),
                passed_along(as_sent(a_state), "row", -1),
                a_state,
            )
            b_state = jax.tree.map(
                lambda part, own: part.astype(own.dtype),
                passed_along(as_sent(b_state), "col", -1),
                b_state,
            )
    keep_mask = c_keep.astype(jnp.float32)
    filtered = total.reshape(MR, BS, NC, BS) * keep_mask[:, None, :, None]
    return filtered.reshape(MR * BS, NC * BS).astype(jnp.bfloat16)


CHUNKS = (32,32,16,16,16,16)
STARTS = tuple(sum(CHUNKS[:n]) for n in range(len(CHUNKS)))
NCH = len(CHUNKS)
EARLY = 8
AHEAD = 3
END_AHEAD = 2
ZERO = NZA
B_INNER = 64
B_COLUMN = 72
DEPTH = NZB * BS
WIDE = NC * BS


def line_kernel(
    a_index_in, a_live_in, b_index_in, c_keep_in, a_ref, b_ref, o_ref,
    own_a, outer_a, inner_a, far_a, own_b, outer_b, own_w, outer_w, own_sum, outer_sum, sum_in,
    own_tab, inner_tab, outer_tab, far_tab, own_bt, outer_bt,
    own_st, inner_st, outer_st, far_st, own_bs, outer_bs,
    local_sem, smem_sem, a_send, a_recv, tab_send, tab_recv,
    b_send, b_recv, bt_send, bt_recv, sum_send, sum_recv,
    a_index, a_live, b_index, c_keep, in_sem,
):
    row = lax.axis_index("row")
    col = lax.axis_index("col")
    is_end = jnp.logical_or(row == 0, row == 3)
    is_middle = jnp.logical_not(is_end)
    outer = jnp.where(row == 1, 0, 3)
    inner = 3 - row
    beside = jnp.where(row == 0, 1, 2)
    panels = (row, inner, 3 - outer, outer)

    def to_row(src, dst, send, recv, target):
        return pltpu.make_async_remote_copy(
            src_ref=src, dst_ref=dst, send_sem=send, recv_sem=recv,
            device_id={"row": target}, device_id_type=pl.DeviceIdType.MESH,
        )

    def to_col(src, dst, send, recv, target):
        return pltpu.make_async_remote_copy(
            src_ref=src, dst_ref=dst, send_sem=send, recv_sem=recv,
            device_id={"col": target}, device_id_type=pl.DeviceIdType.MESH,
        )

    def others():
        return [lax.rem(col + step, 4) for step in range(1, 4)]

    blocks = pl.ds(0, NZA)
    copy_a = pltpu.make_async_copy(a_ref.at[0, 0], own_a.at[blocks], local_sem.at[0])
    copy_b = pltpu.make_async_copy(b_ref.at[0, 0, 0], own_b.at[col], local_sem.at[1])

    barrier = pltpu.get_barrier_semaphore()
    for target in others():
        pl.semaphore_signal(
            barrier, inc=1, device_id={"col": target}, device_id_type=pl.DeviceIdType.MESH
        )

    @pl.when(is_end)
    def _():
        pl.semaphore_signal(
            barrier, inc=1, device_id={"row": beside}, device_id_type=pl.DeviceIdType.MESH
        )

    @pl.when(is_middle)
    def _():
        for target in (outer, inner):
            pl.semaphore_signal(
                barrier, inc=1, device_id={"row": target}, device_id_type=pl.DeviceIdType.MESH
            )

    given = [
        pltpu.make_async_copy(src, dst, in_sem.at[n])
        for n, (src, dst) in enumerate(
            (
                (a_index_in, a_index), (a_live_in, a_live),
                (b_index_in, b_index), (c_keep_in, c_keep),
            )
        )
    ]
    for copy in given:
        copy.start()
    copy_a.start()
    copy_b.start()
    for copy in given:
        copy.wait()
    lane = lax.broadcasted_iota(jnp.int32, (1, BS), 1)
    table = jnp.full((1, BS), ZERO, jnp.int32)
    live = a_live[0, 0]
    for slot in range(NZA):
        place = a_index[0, 0, 0, slot] * KP + a_index[0, 0, 1, slot]
        place = jnp.where(slot < live, place, -1)
        table = jnp.where(lane == place, slot, table)
    for slot in range(NZB):
        table = jnp.where(lane == B_INNER + slot, b_index[0, 0, 0, 0, slot], table)
        table = jnp.where(lane == B_COLUMN + slot, b_index[0, 0, 0, 1, slot], table)
    own_tab[...] = table
    own_bt[col] = table
    blank = jnp.zeros((BS, BS), jnp.bfloat16)
    own_a[ZERO] = blank
    outer_a[ZERO] = blank
    for n in range(NCH):
        inner_a[n][ZERO] = blank[: CHUNKS[n]]
        far_a[n][ZERO] = blank[: CHUNKS[n]]


    @pl.when(is_end)
    def _():
        pl.semaphore_wait(barrier, 4)

    @pl.when(is_middle)
    def _():
        pl.semaphore_wait(barrier, 5)

    def to_smem(src, dst, n):
        return pltpu.make_async_copy(src, dst, smem_sem.at[n])

    def place_b(w_ref, at, blocks_ref, meta, panel):
        for slot in range(NZB):
            column = meta[panel, 0, B_COLUMN + slot]
            block = blocks_ref[panel, slot].astype(jnp.float32)
            for c in range(NC):
                hot = jnp.where(column == c, 1.0, 0.0)
                w_ref[pl.ds(at * DEPTH + slot * BS, BS), pl.ds(c * BS, BS)] = (
                    block * hot
                ).astype(jnp.bfloat16)

    def looked_up(tab, meta, panel):
        places = [meta[panel, 0, B_INNER + slot] for slot in range(NZB)]
        return [[tab[0, r * KP + place] for place in places] for r in range(MR)]

    def picked(a_buf, slots):
        return jnp.concatenate(
            [jnp.concatenate([a_buf[slot] for slot in line], axis=1) for line in slots], axis=0
        )

    def times(x, w_ref, at, count=1):
        product = jnp.dot(
            x, w_ref[pl.ds(at * DEPTH, count * DEPTH), :], preferred_element_type=jnp.float32
        )
        return product.reshape(MR, x.shape[0] // MR, WIDE)

    def store(r, start, size, value):
        for c in range(NC):
            kept = value[:, c * BS : (c + 1) * BS] * c_keep[c, r].astype(jnp.float32)
            o_ref[pl.ds(r * BS + start, size), pl.ds(c * BS, BS)] = kept.astype(jnp.bfloat16)

    @pl.when(is_end)
    def _():
        sends = [
            to_row(own_tab, outer_tab, tab_send.at[0], tab_recv.at[0], beside),
            to_row(own_bt.at[col], outer_bt.at[col], tab_send.at[1], bt_recv.at[1, col], beside),
            to_row(b_ref.at[0, 0, 0], outer_b.at[col], b_send.at[0, 0], b_recv.at[1, col], beside),
        ]
        for n in range(NCH):
            piece = pl.ds(STARTS[n], CHUNKS[n])
            sends.append(
                to_row(
                    a_ref.at[0, 0, :, piece, :], outer_a.at[blocks, piece, :],
                    a_send.at[n], a_recv.at[n], beside,
                )
            )
        for send in sends[: 2 + END_AHEAD]:
            send.start()

        def shared():
            out = []
            for n, target in enumerate(others()):
                out.append(
                    to_col(b_ref.at[0, 0, 0], own_b.at[col], b_send.at[1, n], b_recv.at[0, col], target)
                )
                out.append(
                    to_col(own_tab, own_bt.at[col], bt_send.at[0, n], bt_recv.at[0, col], target)
                )
            return out

        @pl.when(col == row)
        def _():
            for send in shared():
                send.start()

        for n in range(2 + END_AHEAD, len(sends)):
            sends[n - END_AHEAD].wait_send()
            sends[n].start()
        @pl.when(col != row)
        def _():
            to_col(own_bt.at[row], own_bt.at[row], bt_send.at[0, 0], bt_recv.at[0, row], col).wait_recv()
            to_col(own_b.at[row], own_b.at[row], b_send.at[1, 0], b_recv.at[0, row], col).wait_recv()

        loads = [to_smem(own_tab, own_st, 0), to_smem(own_bt, own_bs, 1)]
        for load in loads:
            load.start()
        copy_a.wait()
        copy_b.wait()
        for load in loads:
            load.wait()
        place_b(own_w, 0, own_b, own_bs, row)

        own_sum[...] = times(picked(own_a, looked_up(own_st, own_bs, row)), own_w, 0)
        for n in range(NCH):
            piece = pl.ds(STARTS[n], CHUNKS[n])
            to_row(
                sum_in.at[:, piece, :], sum_in.at[:, piece, :],
                sum_send.at[n], sum_recv.at[n], beside,
            ).wait_recv()
            for r in range(MR):
                store(r, STARTS[n], CHUNKS[n], own_sum[r, piece, :] + sum_in[r, piece, :])
        for send in sends[:2] + sends[-END_AHEAD:]:
            send.wait_send()

        @pl.when(col == row)
        def _():
            for send in shared():
                send.wait_send()

    @pl.when(is_middle)
    def _():
        pieces = [pl.ds(start, size) for start, size in zip(STARTS, CHUNKS)]
        mine = [
            to_row(
                a_ref.at[0, 0, :, pieces[n], :], inner_a[n].at[blocks],
                a_send.at[n], a_recv.at[NCH + n], inner,
            )
            for n in range(NCH)
        ]
        passed = [
            to_row(
                outer_a.at[blocks, pieces[n], :], far_a[n].at[blocks],
                a_send.at[NCH + n], a_recv.at[2 * NCH + n], inner,
            )
            for n in range(NCH)
        ]
        queue = [(send, None) for send in mine[:AHEAD]]
        for n in range(NCH):
            queue.append((passed[n], n))
            queue += [(send, None) for send in mine[AHEAD + n : AHEAD + n + 1]]

        def advance(at):
            queue[at - AHEAD][0].wait_send()
            send, n = queue[at]
            if n is not None:
                part = outer_a.at[blocks, pieces[n], :]
                to_row(part, part, a_send.at[NCH + n], a_recv.at[n], outer).wait_recv()
            send.start()

        sends = [to_row(own_tab, inner_tab, tab_send.at[0], tab_recv.at[1], inner)]
        for n, target in enumerate(others()):
            sends.append(
                to_col(own_tab, own_bt.at[col], bt_send.at[0, n], bt_recv.at[0, col], target)
            )
            sends.append(
                to_col(b_ref.at[0, 0, 0], own_b.at[col], b_send.at[0, n], b_recv.at[0, col], target)
            )
        for send in sends[:1] + mine[:AHEAD] + sends[1:]:
            send.start()

        def passed_b():
            out = []
            for n, target in enumerate(others()):
                out.append(
                    to_col(outer_bt.at[col], outer_bt.at[col], bt_send.at[1, n], bt_recv.at[1, col], target)
                )
                out.append(
                    to_col(outer_b.at[col], outer_b.at[col], b_send.at[1, n], b_recv.at[1, col], target)
                )
            return out

        to_row(outer_tab, outer_tab, tab_send.at[1], tab_recv.at[0], outer).wait_recv()
        onward = [to_row(outer_tab, far_tab, tab_send.at[1], tab_recv.at[2], inner)]
        onward[0].start()
        to_row(outer_bt.at[col], outer_bt.at[col], tab_send.at[1], bt_recv.at[1, col], outer).wait_recv()
        to_row(outer_b.at[col], outer_b.at[col], tab_send.at[1], b_recv.at[1, col], outer).wait_recv()

        @pl.when(col != outer)
        def _():
            for send in passed_b():
                send.start()

        for at in range(AHEAD, EARLY):
            advance(at)

        for source in others():
            to_col(own_bt.at[source], own_bt.at[source], bt_send.at[0, 0], bt_recv.at[0, source], col).wait_recv()
            to_col(own_b.at[source], own_b.at[source], b_send.at[0, 0], b_recv.at[0, source], col).wait_recv()

            @pl.when(source != outer)
            def _():
                to_col(outer_bt.at[source], outer_bt.at[source], bt_send.at[0, 0], bt_recv.at[1, source], col).wait_recv()
                to_col(outer_b.at[source], outer_b.at[source], b_send.at[0, 0], b_recv.at[1, source], col).wait_recv()

        to_row(inner_tab, inner_tab, tab_send.at[1], tab_recv.at[1], inner).wait_recv()
        to_row(far_tab, far_tab, tab_send.at[1], tab_recv.at[2], inner).wait_recv()
        loads = [
            to_smem(src, dst, n)
            for n, (src, dst) in enumerate(
                (
                    (own_tab, own_st), (inner_tab, inner_st), (outer_tab, outer_st),
                    (far_tab, far_st), (own_bt, own_bs), (outer_bt, outer_bs),
                )
            )
        ]
        for load in loads:
            load.start()
        copy_a.wait()
        copy_b.wait()
        for load in loads:
            load.wait()
        tabs = (own_st, inner_st, far_st, outer_st)
        own_slots = [looked_up(tab, own_bs, panel) for tab, panel in zip(tabs, panels)]
        outer_slots = [looked_up(tab, outer_bs, panel) for tab, panel in zip(tabs[:3], panels)]
        for at in range(3):
            place_b(outer_w, at, outer_b, outer_bs, panels[at])
        outer_sum[...] = times(picked(own_a, outer_slots[0]), outer_w, 0)

        def from_inner(n, slots, w_ref):
            x = jnp.concatenate([picked(inner_a[n], slots[1]), picked(far_a[n], slots[2])], axis=1)
            return times(x, w_ref, 1, 2)

        def finish(n):
            total = own_sum[:, pieces[n], :] + from_inner(n, own_slots, own_w)
            for r in range(MR):
                store(r, STARTS[n], CHUNKS[n], total[r])

        at = EARLY
        for n in range(NCH):
            if at < len(queue):
                advance(at)
                at += 1
            to_row(
                inner_a[n].at[blocks], inner_a[n].at[blocks], a_send.at[0], a_recv.at[NCH + n], inner
            ).wait_recv()
            to_row(
                far_a[n].at[blocks], far_a[n].at[blocks], a_send.at[0], a_recv.at[2 * NCH + n], inner
            ).wait_recv()
            outer_sum[:, pieces[n], :] += from_inner(n, outer_slots, outer_w)
            send = to_row(
                outer_sum.at[:, pieces[n], :], sum_in.at[:, pieces[n], :],
                sum_send.at[n], sum_recv.at[n], outer,
            )
            send.start()
            onward.append(send)
            if n == 0:
                for at_w, panel in enumerate(panels):
                    place_b(own_w, at_w, own_b, own_bs, panel)
                own_sum[...] = times(picked(own_a, own_slots[0]), own_w, 0)
            if n == NCH - 2:
                own_sum[...] += times(picked(outer_a, own_slots[3]), own_w, 3)
                for done in range(NCH - 2):
                    finish(done)
        finish(NCH - 2)
        finish(NCH - 1)
        for send in sends + onward + [entry[0] for entry in queue[-AHEAD:]]:
            send.wait_send()

        @pl.when(col != outer)
        def _():
            for send in passed_b():
                send.wait_send()


def line_local(a_blocks, a_index, a_live, b_blocks, b_index, c_keep):
    anywhere = pl.BlockSpec(memory_space=pltpu.HBM)
    dma = pltpu.SemaphoreType.DMA
    panel = pltpu.VMEM((NZA + 1, BS, BS), jnp.bfloat16)
    meta = (1, BS)
    total = pltpu.VMEM((MR, BS, WIDE), jnp.float32)
    return pl.pallas_call(
        line_kernel,
        out_shape=jax.ShapeDtypeStruct((MR * BS, WIDE), jnp.bfloat16),
        in_specs=[anywhere] * 6,
        out_specs=pl.BlockSpec(memory_space=pltpu.VMEM),
        scratch_shapes=[panel] * 2
        + [[pltpu.VMEM((NZA + 1, size, BS), jnp.bfloat16) for size in CHUNKS]] * 2
        + [pltpu.VMEM((4, NZB, BS, BS), jnp.bfloat16)] * 2
        + [pltpu.VMEM((4 * DEPTH, WIDE), jnp.bfloat16), pltpu.VMEM((3 * DEPTH, WIDE), jnp.bfloat16)]
        + [total] * 3
        + [pltpu.VMEM(meta, jnp.int32)] * 4
        + [pltpu.VMEM((4,) + meta, jnp.int32)] * 2
        + [pltpu.SMEM(meta, jnp.int32)] * 4
        + [pltpu.SMEM((4,) + meta, jnp.int32)] * 2
        + [
            dma((2,)), dma((6,)),
            dma((2 * NCH,)), dma((3 * NCH,)), dma((2,)), dma((3,)),
            dma((2, 3)), dma((2, 4)), dma((2, 3)), dma((2, 4)),
            dma((NCH,)), dma((NCH,)),
        ]
        + [pltpu.SMEM(one.shape, jnp.int32) for one in (a_index, a_live, b_index, c_keep.T)]
        + [dma((4,))],
        compiler_params=pltpu.CompilerParams(
            collective_id=0, has_side_effects=True, vmem_limit_bytes=54630 * 1024
        ),
    )(a_index, a_live, b_index, c_keep.T, a_blocks, b_blocks)


def solution(mesh):
    placed = (
        P(("groups", "row"), "col", None, None, None),
        P(("groups", "row"), "col", None, None),
        P(("groups", "row"), "col"),
        P(("groups", "row"), "col", None, None, None, None),
        P(("groups", "row"), "col", None, None, None),
        P(("groups", "col"), "row"),
    )
    short_line = mesh.shape["row"] == 4 and mesh.shape["col"] == 4
    return jax.shard_map(
        line_local if short_line else local, mesh=mesh, in_specs=placed, out_specs=P(("groups", "col"), "row"), check_vma=False
    )
```

```python
import jax
import jax.numpy as jnp
from jax import lax
from jax.experimental import pallas as pl
from jax.experimental.pallas import tpu as pltpu
from jax.sharding import PartitionSpec as P

BS = 128
MR = 4
NC = 2
KP = 8
NZA = 16
NZB = 3


def as_sent(array):
    return jax.tree.map(lambda a: a.astype(jnp.bfloat16) if a.dtype == jnp.float32 else a, array)


def passed_along(value, axis, steps):
    count = lax.axis_size(axis)
    pairs = [(source, (source + steps) % count) for source in range(count)]
    return lax.ppermute(value, axis, pairs)


def panel_product(total, first_blocks, first_index, first_live, second_blocks, second_index):
    slot_ids = second_index[0] * NC + second_index[1]
    slot_range = jnp.arange(KP * NC, dtype=jnp.int32)
    picker = (slot_range[:, None] == slot_ids[None, :]).astype(jnp.bfloat16).reshape(KP, NC, NZB)
    dense_b = jnp.einsum(
        "kcz,zuv->kucv", picker, second_blocks, preferred_element_type=jnp.bfloat16
    )
    dense_b = dense_b.reshape(KP * BS, NC * BS)
    live_mask = (jnp.arange(NZA, dtype=jnp.int32) < first_live).astype(jnp.bfloat16)
    row_hot = (jnp.arange(MR, dtype=jnp.int32)[:, None] == first_index[0][None, :]).astype(
        jnp.bfloat16
    )
    inner_hot = (jnp.arange(KP, dtype=jnp.int32)[:, None] == first_index[1][None, :]).astype(
        jnp.bfloat16
    )
    placer = row_hot[:, None, :] * inner_hot[None, :, :] * live_mask[None, None, :]
    dense_a = jnp.einsum("rkz,zuv->rukv", placer, first_blocks, preferred_element_type=jnp.bfloat16)
    dense_a = dense_a.reshape(MR * BS, KP * BS)
    return total + jnp.dot(dense_a, dense_b, preferred_element_type=jnp.float32)


def local(a_blocks, a_index, a_live, b_blocks, b_index, c_keep):
    row_count = lax.axis_size("row")
    col_count = lax.axis_size("col")
    row_pos = lax.axis_index("row")
    col_pos = lax.axis_index("col")
    tick_total = min(6, row_count)
    bit_total = col_count.bit_length() - 1
    a_state = (a_blocks, a_index, a_live)
    for bit_pos in range(bit_total):
        shifted = jax.tree.map(
            lambda part, own: part.astype(own.dtype),
            passed_along(as_sent(a_state), "row", -(1 << bit_pos)),
            a_state,
        )
        take_bit = col_pos // (1 << bit_pos) % 2 == 1
        a_state = jax.tree.map(
            lambda incoming, current: jnp.where(take_bit, incoming, current), shifted, a_state
        )
    skew_amount = row_pos % col_count
    b_state = (b_blocks, b_index)
    for bit_pos in range(bit_total):
        shifted = jax.tree.map(
            lambda part, own: part.astype(own.dtype),
            passed_along(as_sent(b_state), "col", -(1 << bit_pos)),
            b_state,
        )
        take_bit = skew_amount // (1 << bit_pos) % 2 == 1
        b_state = jax.tree.map(
            lambda incoming, current: jnp.where(take_bit, incoming, current), shifted, b_state
        )
    total = jnp.zeros((MR * BS, NC * BS), jnp.float32)
    for tick_no in range(tick_total):
        panel_id = (col_pos + row_pos + tick_no) % row_count
        depth_id = panel_id // col_count
        group_blocks = b_state[0][0, 0]
        group_index = b_state[1][0, 0]
        second_blocks = lax.dynamic_index_in_dim(group_blocks, depth_id, 0, keepdims=False)
        second_index = lax.dynamic_index_in_dim(group_index, depth_id, 0, keepdims=False)
        first_blocks, first_index, first_live = a_state
        total = panel_product(
            total,
            first_blocks[0, 0],
            first_index[0, 0],
            first_live[0, 0],
            second_blocks,
            second_index,
        )
        if tick_no + 1 < tick_total:
            a_state = jax.tree.map(
                lambda part, own: part.astype(own.dtype),
                passed_along(as_sent(a_state), "row", -1),
                a_state,
            )
            b_state = jax.tree.map(
                lambda part, own: part.astype(own.dtype),
                passed_along(as_sent(b_state), "col", -1),
                b_state,
            )
    keep_mask = c_keep.astype(jnp.float32)
    filtered = total.reshape(MR, BS, NC, BS) * keep_mask[:, None, :, None]
    return filtered.reshape(MR * BS, NC * BS).astype(jnp.bfloat16)


CHUNKS = (32,32,16,16,16,16)
STARTS = tuple(sum(CHUNKS[:n]) for n in range(len(CHUNKS)))
NCH = len(CHUNKS)
EARLY = 8
AHEAD = 3
END_AHEAD = 2
ZERO = NZA
B_INNER = 64
B_COLUMN = 72
DEPTH = NZB * BS
WIDE = NC * BS


def line_kernel(
    a_index_in, a_live_in, b_index_in, c_keep_in, a_ref, b_ref, o_ref,
    own_a, outer_a, inner_a, far_a, own_b, outer_b, own_w, outer_w, own_sum, outer_sum, sum_in,
    own_tab, inner_tab, outer_tab, far_tab, own_bt, outer_bt,
    own_st, inner_st, outer_st, far_st, own_bs, outer_bs,
    local_sem, smem_sem, a_send, a_recv, tab_send, tab_recv,
    b_send, b_recv, bt_send, bt_recv, sum_send, sum_recv,
    a_index, a_live, b_index, c_keep, in_sem,
):
    row = lax.axis_index("row")
    col = lax.axis_index("col")
    is_end = jnp.logical_or(row == 0, row == 3)
    is_middle = jnp.logical_not(is_end)
    outer = jnp.where(row == 1, 0, 3)
    inner = 3 - row
    beside = jnp.where(row == 0, 1, 2)
    panels = (row, inner, 3 - outer, outer)

    def to_row(src, dst, send, recv, target):
        return pltpu.make_async_remote_copy(
            src_ref=src, dst_ref=dst, send_sem=send, recv_sem=recv,
            device_id={"row": target}, device_id_type=pl.DeviceIdType.MESH,
        )

    def to_col(src, dst, send, recv, target):
        return pltpu.make_async_remote_copy(
            src_ref=src, dst_ref=dst, send_sem=send, recv_sem=recv,
            device_id={"col": target}, device_id_type=pl.DeviceIdType.MESH,
        )

    def others():
        return [lax.rem(col + step, 4) for step in range(1, 4)]

    blocks = pl.ds(0, NZA)
    copy_a = pltpu.make_async_copy(a_ref.at[0, 0], own_a.at[blocks], local_sem.at[0])
    copy_b = pltpu.make_async_copy(b_ref.at[0, 0, 0], own_b.at[col], local_sem.at[1])

    barrier = pltpu.get_barrier_semaphore()
    for target in others():
        pl.semaphore_signal(
            barrier, inc=1, device_id={"col": target}, device_id_type=pl.DeviceIdType.MESH
        )

    @pl.when(is_end)
    def _():
        pl.semaphore_signal(
            barrier, inc=1, device_id={"row": beside}, device_id_type=pl.DeviceIdType.MESH
        )

    @pl.when(is_middle)
    def _():
        for target in (outer, inner):
            pl.semaphore_signal(
                barrier, inc=1, device_id={"row": target}, device_id_type=pl.DeviceIdType.MESH
            )

    given = [
        pltpu.make_async_copy(src, dst, in_sem.at[n])
        for n, (src, dst) in enumerate(
            (
                (a_index_in, a_index), (a_live_in, a_live),
                (b_index_in, b_index), (c_keep_in, c_keep),
            )
        )
    ]
    for copy in given:
        copy.start()
    copy_a.start()
    copy_b.start()
    for copy in given:
        copy.wait()
    lane = lax.broadcasted_iota(jnp.int32, (1, BS), 1)
    table = jnp.full((1, BS), ZERO, jnp.int32)
    live = a_live[0, 0]
    for slot in range(NZA):
        place = a_index[0, 0, 0, slot] * KP + a_index[0, 0, 1, slot]
        place = jnp.where(slot < live, place, -1)
        table = jnp.where(lane == place, slot, table)
    for slot in range(NZB):
        table = jnp.where(lane == B_INNER + slot, b_index[0, 0, 0, 0, slot], table)
        table = jnp.where(lane == B_COLUMN + slot, b_index[0, 0, 0, 1, slot], table)
    own_tab[...] = table
    own_bt[col] = table
    blank = jnp.zeros((BS, BS), jnp.bfloat16)
    own_a[ZERO] = blank
    outer_a[ZERO] = blank
    for n in range(NCH):
        inner_a[n][ZERO] = blank[: CHUNKS[n]]
        far_a[n][ZERO] = blank[: CHUNKS[n]]


    @pl.when(is_end)
    def _():
        pl.semaphore_wait(barrier, 4)

    @pl.when(is_middle)
    def _():
        pl.semaphore_wait(barrier, 5)

    def to_smem(src, dst, n):
        return pltpu.make_async_copy(src, dst, smem_sem.at[n])

    def place_b(w_ref, at, blocks_ref, meta, panel):
        for slot in range(NZB):
            column = meta[panel, 0, B_COLUMN + slot]
            block = blocks_ref[panel, slot].astype(jnp.float32)
            for c in range(NC):
                hot = jnp.where(column == c, 1.0, 0.0)
                w_ref[pl.ds(at * DEPTH + slot * BS, BS), pl.ds(c * BS, BS)] = (
                    block * hot
                ).astype(jnp.bfloat16)

    def looked_up(tab, meta, panel):
        places = [meta[panel, 0, B_INNER + slot] for slot in range(NZB)]
        return [[tab[0, r * KP + place] for place in places] for r in range(MR)]

    def picked(a_buf, slots):
        return jnp.concatenate(
            [jnp.concatenate([a_buf[slot] for slot in line], axis=1) for line in slots], axis=0
        )

    def times(x, w_ref, at, count=1):
        product = jnp.dot(
            x, w_ref[pl.ds(at * DEPTH, count * DEPTH), :], preferred_element_type=jnp.float32
        )
        return product.reshape(MR, x.shape[0] // MR, WIDE)

    def store(r, start, size, value):
        for c in range(NC):
            kept = value[:, c * BS : (c + 1) * BS] * c_keep[c, r].astype(jnp.float32)
            o_ref[pl.ds(r * BS + start, size), pl.ds(c * BS, BS)] = kept.astype(jnp.bfloat16)

    @pl.when(is_end)
    def _():
        sends = [
            to_row(own_tab, outer_tab, tab_send.at[0], tab_recv.at[0], beside),
            to_row(own_bt.at[col], outer_bt.at[col], tab_send.at[1], bt_recv.at[1, col], beside),
            to_row(b_ref.at[0, 0, 0], outer_b.at[col], b_send.at[0, 0], b_recv.at[1, col], beside),
        ]
        for n in range(NCH):
            piece = pl.ds(STARTS[n], CHUNKS[n])
            sends.append(
                to_row(
                    a_ref.at[0, 0, :, piece, :], outer_a.at[blocks, piece, :],
                    a_send.at[n], a_recv.at[n], beside,
                )
            )
        for send in sends[: 2 + END_AHEAD]:
            send.start()

        def shared():
            out = []
            for n, target in enumerate(others()):
                out.append(
                    to_col(b_ref.at[0, 0, 0], own_b.at[col], b_send.at[1, n], b_recv.at[0, col], target)
                )
                out.append(
                    to_col(own_tab, own_bt.at[col], bt_send.at[0, n], bt_recv.at[0, col], target)
                )
            return out

        @pl.when(col == row)
        def _():
            for send in shared():
                send.start()

        for n in range(2 + END_AHEAD, len(sends)):
            sends[n - END_AHEAD].wait_send()
            sends[n].start()
        @pl.when(col != row)
        def _():
            to_col(own_bt.at[row], own_bt.at[row], bt_send.at[0, 0], bt_recv.at[0, row], col).wait_recv()
            to_col(own_b.at[row], own_b.at[row], b_send.at[1, 0], b_recv.at[0, row], col).wait_recv()

        loads = [to_smem(own_tab, own_st, 0), to_smem(own_bt, own_bs, 1)]
        for load in loads:
            load.start()
        copy_a.wait()
        copy_b.wait()
        for load in loads:
            load.wait()
        place_b(own_w, 0, own_b, own_bs, row)

        own_sum[...] = times(picked(own_a, looked_up(own_st, own_bs, row)), own_w, 0)
        for n in range(NCH):
            piece = pl.ds(STARTS[n], CHUNKS[n])
            to_row(
                sum_in.at[:, piece, :], sum_in.at[:, piece, :],
                sum_send.at[n], sum_recv.at[n], beside,
            ).wait_recv()
            for r in range(MR):
                store(r, STARTS[n], CHUNKS[n], own_sum[r, piece, :] + sum_in[r, piece, :])
        for send in sends[:2] + sends[-END_AHEAD:]:
            send.wait_send()

        @pl.when(col == row)
        def _():
            for send in shared():
                send.wait_send()

    @pl.when(is_middle)
    def _():
        pieces = [pl.ds(start, size) for start, size in zip(STARTS, CHUNKS)]
        mine = [
            to_row(
                a_ref.at[0, 0, :, pieces[n], :], inner_a[n].at[blocks],
                a_send.at[n], a_recv.at[NCH + n], inner,
            )
            for n in range(NCH)
        ]
        passed = [
            to_row(
                outer_a.at[blocks, pieces[n], :], far_a[n].at[blocks],
                a_send.at[NCH + n], a_recv.at[2 * NCH + n], inner,
            )
            for n in range(NCH)
        ]
        queue = [(send, None) for send in mine[:AHEAD]]
        for n in range(NCH):
            queue.append((passed[n], n))
            queue += [(send, None) for send in mine[AHEAD + n : AHEAD + n + 1]]

        def advance(at):
            queue[at - AHEAD][0].wait_send()
            send, n = queue[at]
            if n is not None:
                part = outer_a.at[blocks, pieces[n], :]
                to_row(part, part, a_send.at[NCH + n], a_recv.at[n], outer).wait_recv()
            send.start()

        sends = [to_row(own_tab, inner_tab, tab_send.at[0], tab_recv.at[1], inner)]
        for n, target in enumerate(others()):
            sends.append(
                to_col(own_tab, own_bt.at[col], bt_send.at[0, n], bt_recv.at[0, col], target)
            )
            sends.append(
                to_col(b_ref.at[0, 0, 0], own_b.at[col], b_send.at[0, n], b_recv.at[0, col], target)
            )
        for send in sends[:1] + mine[:AHEAD] + sends[1:]:
            send.start()

        def passed_b():
            out = []
            for n, target in enumerate(others()):
                out.append(
                    to_col(outer_bt.at[col], outer_bt.at[col], bt_send.at[1, n], bt_recv.at[1, col], target)
                )
                out.append(
                    to_col(outer_b.at[col], outer_b.at[col], b_send.at[1, n], b_recv.at[1, col], target)
                )
            return out

        to_row(outer_tab, outer_tab, tab_send.at[1], tab_recv.at[0], outer).wait_recv()
        onward = [to_row(outer_tab, far_tab, tab_send.at[1], tab_recv.at[2], inner)]
        onward[0].start()
        to_row(outer_bt.at[col], outer_bt.at[col], tab_send.at[1], bt_recv.at[1, col], outer).wait_recv()
        to_row(outer_b.at[col], outer_b.at[col], tab_send.at[1], b_recv.at[1, col], outer).wait_recv()

        @pl.when(col != outer)
        def _():
            for send in passed_b():
                send.start()

        for at in range(AHEAD, EARLY):
            advance(at)

        for source in others():
            to_col(own_bt.at[source], own_bt.at[source], bt_send.at[0, 0], bt_recv.at[0, source], col).wait_recv()
            to_col(own_b.at[source], own_b.at[source], b_send.at[0, 0], b_recv.at[0, source], col).wait_recv()

            @pl.when(source != outer)
            def _():
                to_col(outer_bt.at[source], outer_bt.at[source], bt_send.at[0, 0], bt_recv.at[1, source], col).wait_recv()
                to_col(outer_b.at[source], outer_b.at[source], b_send.at[0, 0], b_recv.at[1, source], col).wait_recv()

        to_row(inner_tab, inner_tab, tab_send.at[1], tab_recv.at[1], inner).wait_recv()
        to_row(far_tab, far_tab, tab_send.at[1], tab_recv.at[2], inner).wait_recv()
        loads = [
            to_smem(src, dst, n)
            for n, (src, dst) in enumerate(
                (
                    (own_tab, own_st), (inner_tab, inner_st), (outer_tab, outer_st),
                    (far_tab, far_st), (own_bt, own_bs), (outer_bt, outer_bs),
                )
            )
        ]
        for load in loads:
            load.start()
        copy_a.wait()
        copy_b.wait()
        for load in loads:
            load.wait()
        tabs = (own_st, inner_st, far_st, outer_st)
        own_slots = [looked_up(tab, own_bs, panel) for tab, panel in zip(tabs, panels)]
        outer_slots = [looked_up(tab, outer_bs, panel) for tab, panel in zip(tabs[:3], panels)]
        for at in range(3):
            place_b(outer_w, at, outer_b, outer_bs, panels[at])
        outer_sum[...] = times(picked(own_a, outer_slots[0]), outer_w, 0)

        def from_inner(n, slots, w_ref):
            x = jnp.concatenate([picked(inner_a[n], slots[1]), picked(far_a[n], slots[2])], axis=1)
            return times(x, w_ref, 1, 2)

        def finish(n):
            total = own_sum[:, pieces[n], :] + from_inner(n, own_slots, own_w)
            for r in range(MR):
                store(r, STARTS[n], CHUNKS[n], total[r])

        at = EARLY
        for n in range(NCH):
            if at < len(queue):
                advance(at)
                at += 1
            to_row(
                inner_a[n].at[blocks], inner_a[n].at[blocks], a_send.at[0], a_recv.at[NCH + n], inner
            ).wait_recv()
            to_row(
                far_a[n].at[blocks], far_a[n].at[blocks], a_send.at[0], a_recv.at[2 * NCH + n], inner
            ).wait_recv()
            outer_sum[:, pieces[n], :] += from_inner(n, outer_slots, outer_w)
            send = to_row(
                outer_sum.at[:, pieces[n], :], sum_in.at[:, pieces[n], :],
                sum_send.at[n], sum_recv.at[n], outer,
            )
            send.start()
            onward.append(send)
            if n == 0:
                for at_w, panel in enumerate(panels):
                    place_b(own_w, at_w, own_b, own_bs, panel)
                own_sum[...] = times(picked(own_a, own_slots[0]), own_w, 0)
            if n == NCH - 2:
                own_sum[...] += times(picked(outer_a, own_slots[3]), own_w, 3)
                for done in range(NCH - 2):
                    finish(done)
        finish(NCH - 2)
        finish(NCH - 1)
        for send in sends + onward + [entry[0] for entry in queue[-AHEAD:]]:
            send.wait_send()

        @pl.when(col != outer)
        def _():
            for send in passed_b():
                send.wait_send()


def line_local(a_blocks, a_index, a_live, b_blocks, b_index, c_keep):
    anywhere = pl.BlockSpec(memory_space=pltpu.HBM)
    dma = pltpu.SemaphoreType.DMA
    panel = pltpu.VMEM((NZA + 1, BS, BS), jnp.bfloat16)
    meta = (1, BS)
    total = pltpu.VMEM((MR, BS, WIDE), jnp.float32)
    return pl.pallas_call(
        line_kernel,
        out_shape=pltpu.VMEM((MR * BS, WIDE), jnp.bfloat16),
        in_specs=[anywhere] * 6,
        out_specs=pl.BlockSpec(memory_space=pltpu.VMEM),
        scratch_shapes=[panel] * 2
        + [[pltpu.VMEM((NZA + 1, size, BS), jnp.bfloat16) for size in CHUNKS]] * 2
        + [pltpu.VMEM((4, NZB, BS, BS), jnp.bfloat16)] * 2
        + [pltpu.VMEM((4 * DEPTH, WIDE), jnp.bfloat16), pltpu.VMEM((3 * DEPTH, WIDE), jnp.bfloat16)]
        + [total] * 3
        + [pltpu.VMEM(meta, jnp.int32)] * 4
        + [pltpu.VMEM((4,) + meta, jnp.int32)] * 2
        + [pltpu.SMEM(meta, jnp.int32)] * 4
        + [pltpu.SMEM((4,) + meta, jnp.int32)] * 2
        + [
            dma((2,)), dma((6,)),
            dma((2 * NCH,)), dma((3 * NCH,)), dma((2,)), dma((3,)),
            dma((2, 3)), dma((2, 4)), dma((2, 3)), dma((2, 4)),
            dma((NCH,)), dma((NCH,)),
        ]
        + [pltpu.SMEM(one.shape, jnp.int32) for one in (a_index, a_live, b_index, c_keep.T)]
        + [dma((4,))],
        compiler_params=pltpu.CompilerParams(
            collective_id=0, has_side_effects=True, vmem_limit_bytes=60 * 1024 * 1024
        ),
    )(a_index, a_live, b_index, c_keep.T, a_blocks, b_blocks)


def solution(mesh):
    placed = (
        P(("groups", "row"), "col", None, None, None),
        P(("groups", "row"), "col", None, None),
        P(("groups", "row"), "col"),
        P(("groups", "row"), "col", None, None, None, None),
        P(("groups", "row"), "col", None, None, None),
        P(("groups", "col"), "row"),
    )
    short_line = mesh.shape["row"] == 4 and mesh.shape["col"] == 4
    return jax.shard_map(
        line_local if short_line else local, mesh=mesh, in_specs=placed, out_specs=P(("groups", "col"), "row"), check_vma=False
    )
```

```python
import jax
import jax.numpy as jnp
from jax import lax
from jax.experimental import pallas as pl
from jax.experimental.pallas import tpu as pltpu
from jax.sharding import PartitionSpec as P

BS = 128
MR = 4
NC = 2
KP = 8
NZA = 16
NZB = 3


def as_sent(array):
    return jax.tree.map(lambda a: a.astype(jnp.bfloat16) if a.dtype == jnp.float32 else a, array)


def passed_along(value, axis, steps):
    count = lax.axis_size(axis)
    pairs = [(source, (source + steps) % count) for source in range(count)]
    return lax.ppermute(value, axis, pairs)


def panel_product(total, first_blocks, first_index, first_live, second_blocks, second_index):
    slot_ids = second_index[0] * NC + second_index[1]
    slot_range = jnp.arange(KP * NC, dtype=jnp.int32)
    picker = (slot_range[:, None] == slot_ids[None, :]).astype(jnp.bfloat16).reshape(KP, NC, NZB)
    dense_b = jnp.einsum(
        "kcz,zuv->kucv", picker, second_blocks, preferred_element_type=jnp.bfloat16
    )
    dense_b = dense_b.reshape(KP * BS, NC * BS)
    live_mask = (jnp.arange(NZA, dtype=jnp.int32) < first_live).astype(jnp.bfloat16)
    row_hot = (jnp.arange(MR, dtype=jnp.int32)[:, None] == first_index[0][None, :]).astype(
        jnp.bfloat16
    )
    inner_hot = (jnp.arange(KP, dtype=jnp.int32)[:, None] == first_index[1][None, :]).astype(
        jnp.bfloat16
    )
    placer = row_hot[:, None, :] * inner_hot[None, :, :] * live_mask[None, None, :]
    dense_a = jnp.einsum("rkz,zuv->rukv", placer, first_blocks, preferred_element_type=jnp.bfloat16)
    dense_a = dense_a.reshape(MR * BS, KP * BS)
    return total + jnp.dot(dense_a, dense_b, preferred_element_type=jnp.float32)


def local(a_blocks, a_index, a_live, b_blocks, b_index, c_keep):
    row_count = lax.axis_size("row")
    col_count = lax.axis_size("col")
    row_pos = lax.axis_index("row")
    col_pos = lax.axis_index("col")
    tick_total = min(6, row_count)
    bit_total = col_count.bit_length() - 1
    a_state = (a_blocks, a_index, a_live)
    for bit_pos in range(bit_total):
        shifted = jax.tree.map(
            lambda part, own: part.astype(own.dtype),
            passed_along(as_sent(a_state), "row", -(1 << bit_pos)),
            a_state,
        )
        take_bit = col_pos // (1 << bit_pos) % 2 == 1
        a_state = jax.tree.map(
            lambda incoming, current: jnp.where(take_bit, incoming, current), shifted, a_state
        )
    skew_amount = row_pos % col_count
    b_state = (b_blocks, b_index)
    for bit_pos in range(bit_total):
        shifted = jax.tree.map(
            lambda part, own: part.astype(own.dtype),
            passed_along(as_sent(b_state), "col", -(1 << bit_pos)),
            b_state,
        )
        take_bit = skew_amount // (1 << bit_pos) % 2 == 1
        b_state = jax.tree.map(
            lambda incoming, current: jnp.where(take_bit, incoming, current), shifted, b_state
        )
    total = jnp.zeros((MR * BS, NC * BS), jnp.float32)
    for tick_no in range(tick_total):
        panel_id = (col_pos + row_pos + tick_no) % row_count
        depth_id = panel_id // col_count
        group_blocks = b_state[0][0, 0]
        group_index = b_state[1][0, 0]
        second_blocks = lax.dynamic_index_in_dim(group_blocks, depth_id, 0, keepdims=False)
        second_index = lax.dynamic_index_in_dim(group_index, depth_id, 0, keepdims=False)
        first_blocks, first_index, first_live = a_state
        total = panel_product(
            total,
            first_blocks[0, 0],
            first_index[0, 0],
            first_live[0, 0],
            second_blocks,
            second_index,
        )
        if tick_no + 1 < tick_total:
            a_state = jax.tree.map(
                lambda part, own: part.astype(own.dtype),
                passed_along(as_sent(a_state), "row", -1),
                a_state,
            )
            b_state = jax.tree.map(
                lambda part, own: part.astype(own.dtype),
                passed_along(as_sent(b_state), "col", -1),
                b_state,
            )
    keep_mask = c_keep.astype(jnp.float32)
    filtered = total.reshape(MR, BS, NC, BS) * keep_mask[:, None, :, None]
    return filtered.reshape(MR * BS, NC * BS).astype(jnp.bfloat16)


CHUNKS = (32,32,16,16,16,16)
STARTS = tuple(sum(CHUNKS[:n]) for n in range(len(CHUNKS)))
NCH = len(CHUNKS)
EARLY = 8
AHEAD = 3
END_AHEAD = 1
ZERO = NZA
B_INNER = 64
B_COLUMN = 72
DEPTH = NZB * BS
WIDE = NC * BS


def line_kernel(
    a_index_in, a_live_in, b_index_in, c_keep_in, a_ref, b_ref, o_ref,
    own_a, outer_a, inner_a, far_a, own_b, outer_b, own_w, outer_w, own_sum, outer_sum, sum_in,
    own_tab, inner_tab, outer_tab, far_tab, own_bt, outer_bt,
    own_st, inner_st, outer_st, far_st, own_bs, outer_bs,
    local_sem, smem_sem, a_send, a_recv, tab_send, tab_recv,
    b_send, b_recv, bt_send, bt_recv, sum_send, sum_recv,
    a_index, a_live, b_index, c_keep, in_sem,
):
    row = lax.axis_index("row")
    col = lax.axis_index("col")
    is_end = jnp.logical_or(row == 0, row == 3)
    is_middle = jnp.logical_not(is_end)
    outer = jnp.where(row == 1, 0, 3)
    inner = 3 - row
    beside = jnp.where(row == 0, 1, 2)
    panels = (row, inner, 3 - outer, outer)

    def to_row(src, dst, send, recv, target):
        return pltpu.make_async_remote_copy(
            src_ref=src, dst_ref=dst, send_sem=send, recv_sem=recv,
            device_id={"row": target}, device_id_type=pl.DeviceIdType.MESH,
        )

    def to_col(src, dst, send, recv, target):
        return pltpu.make_async_remote_copy(
            src_ref=src, dst_ref=dst, send_sem=send, recv_sem=recv,
            device_id={"col": target}, device_id_type=pl.DeviceIdType.MESH,
        )

    def others():
        return [lax.rem(col + step, 4) for step in range(1, 4)]

    blocks = pl.ds(0, NZA)
    copy_a = pltpu.make_async_copy(a_ref.at[0, 0], own_a.at[blocks], local_sem.at[0])
    copy_b = pltpu.make_async_copy(b_ref.at[0, 0, 0], own_b.at[col], local_sem.at[1])

    barrier = pltpu.get_barrier_semaphore()
    for target in others():
        pl.semaphore_signal(
            barrier, inc=1, device_id={"col": target}, device_id_type=pl.DeviceIdType.MESH
        )

    @pl.when(is_end)
    def _():
        pl.semaphore_signal(
            barrier, inc=1, device_id={"row": beside}, device_id_type=pl.DeviceIdType.MESH
        )

    @pl.when(is_middle)
    def _():
        for target in (outer, inner):
            pl.semaphore_signal(
                barrier, inc=1, device_id={"row": target}, device_id_type=pl.DeviceIdType.MESH
            )

    given = [
        pltpu.make_async_copy(src, dst, in_sem.at[n])
        for n, (src, dst) in enumerate(
            (
                (a_index_in, a_index), (a_live_in, a_live),
                (b_index_in, b_index), (c_keep_in, c_keep),
            )
        )
    ]
    for copy in given:
        copy.start()
    copy_a.start()
    copy_b.start()
    for copy in given:
        copy.wait()
    lane = lax.broadcasted_iota(jnp.int32, (1, BS), 1)
    table = jnp.full((1, BS), ZERO, jnp.int32)
    live = a_live[0, 0]
    for slot in range(NZA):
        place = a_index[0, 0, 0, slot] * KP + a_index[0, 0, 1, slot]
        place = jnp.where(slot < live, place, -1)
        table = jnp.where(lane == place, slot, table)
    for slot in range(NZB):
        table = jnp.where(lane == B_INNER + slot, b_index[0, 0, 0, 0, slot], table)
        table = jnp.where(lane == B_COLUMN + slot, b_index[0, 0, 0, 1, slot], table)
    own_tab[...] = table
    own_bt[col] = table
    blank = jnp.zeros((BS, BS), jnp.bfloat16)
    own_a[ZERO] = blank
    outer_a[ZERO] = blank
    for n in range(NCH):
        inner_a[n][ZERO] = blank[: CHUNKS[n]]
        far_a[n][ZERO] = blank[: CHUNKS[n]]


    @pl.when(is_end)
    def _():
        pl.semaphore_wait(barrier, 4)

    @pl.when(is_middle)
    def _():
        pl.semaphore_wait(barrier, 5)

    def to_smem(src, dst, n):
        return pltpu.make_async_copy(src, dst, smem_sem.at[n])

    def place_b(w_ref, at, blocks_ref, meta, panel):
        for slot in range(NZB):
            column = meta[panel, 0, B_COLUMN + slot]
            block = blocks_ref[panel, slot].astype(jnp.float32)
            for c in range(NC):
                hot = jnp.where(column == c, 1.0, 0.0)
                w_ref[pl.ds(at * DEPTH + slot * BS, BS), pl.ds(c * BS, BS)] = (
                    block * hot
                ).astype(jnp.bfloat16)

    def looked_up(tab, meta, panel):
        places = [meta[panel, 0, B_INNER + slot] for slot in range(NZB)]
        return [[tab[0, r * KP + place] for place in places] for r in range(MR)]

    def picked(a_buf, slots):
        return jnp.concatenate(
            [jnp.concatenate([a_buf[slot] for slot in line], axis=1) for line in slots], axis=0
        )

    def times(x, w_ref, at, count=1):
        product = jnp.dot(
            x, w_ref[pl.ds(at * DEPTH, count * DEPTH), :], preferred_element_type=jnp.float32
        )
        return product.reshape(MR, x.shape[0] // MR, WIDE)

    def store(r, start, size, value):
        for c in range(NC):
            kept = value[:, c * BS : (c + 1) * BS] * c_keep[c, r].astype(jnp.float32)
            o_ref[pl.ds(r * BS + start, size), pl.ds(c * BS, BS)] = kept.astype(jnp.bfloat16)

    @pl.when(is_end)
    def _():
        sends = [
            to_row(own_tab, outer_tab, tab_send.at[0], tab_recv.at[0], beside),
            to_row(own_bt.at[col], outer_bt.at[col], tab_send.at[1], bt_recv.at[1, col], beside),
            to_row(b_ref.at[0, 0, 0], outer_b.at[col], b_send.at[0, 0], b_recv.at[1, col], beside),
        ]
        for n in range(NCH):
            piece = pl.ds(STARTS[n], CHUNKS[n])
            sends.append(
                to_row(
                    a_ref.at[0, 0, :, piece, :], outer_a.at[blocks, piece, :],
                    a_send.at[n], a_recv.at[n], beside,
                )
            )
        for send in sends[: 2 + END_AHEAD]:
            send.start()

        def shared():
            out = []
            for n, target in enumerate(others()):
                out.append(
                    to_col(b_ref.at[0, 0, 0], own_b.at[col], b_send.at[1, n], b_recv.at[0, col], target)
                )
                out.append(
                    to_col(own_tab, own_bt.at[col], bt_send.at[0, n], bt_recv.at[0, col], target)
                )
            return out

        @pl.when(col == row)
        def _():
            for send in shared():
                send.start()

        for n in range(2 + END_AHEAD, len(sends)):
            sends[n - END_AHEAD].wait_send()
            sends[n].start()
        @pl.when(col != row)
        def _():
            to_col(own_bt.at[row], own_bt.at[row], bt_send.at[0, 0], bt_recv.at[0, row], col).wait_recv()
            to_col(own_b.at[row], own_b.at[row], b_send.at[1, 0], b_recv.at[0, row], col).wait_recv()

        loads = [to_smem(own_tab, own_st, 0), to_smem(own_bt, own_bs, 1)]
        for load in loads:
            load.start()
        copy_a.wait()
        copy_b.wait()
        for load in loads:
            load.wait()
        place_b(own_w, 0, own_b, own_bs, row)

        own_sum[...] = times(picked(own_a, looked_up(own_st, own_bs, row)), own_w, 0)
        for n in range(NCH):
            piece = pl.ds(STARTS[n], CHUNKS[n])
            to_row(
                sum_in.at[:, piece, :], sum_in.at[:, piece, :],
                sum_send.at[n], sum_recv.at[n], beside,
            ).wait_recv()
            for r in range(MR):
                store(r, STARTS[n], CHUNKS[n], own_sum[r, piece, :] + sum_in[r, piece, :])
        for send in sends[:2] + sends[-END_AHEAD:]:
            send.wait_send()

        @pl.when(col == row)
        def _():
            for send in shared():
                send.wait_send()

    @pl.when(is_middle)
    def _():
        pieces = [pl.ds(start, size) for start, size in zip(STARTS, CHUNKS)]
        mine = [
            to_row(
                a_ref.at[0, 0, :, pieces[n], :], inner_a[n].at[blocks],
                a_send.at[n], a_recv.at[NCH + n], inner,
            )
            for n in range(NCH)
        ]
        passed = [
            to_row(
                outer_a.at[blocks, pieces[n], :], far_a[n].at[blocks],
                a_send.at[NCH + n], a_recv.at[2 * NCH + n], inner,
            )
            for n in range(NCH)
        ]
        queue = [(send, None) for send in mine[:AHEAD]]
        for n in range(NCH):
            queue.append((passed[n], n))
            queue += [(send, None) for send in mine[AHEAD + n : AHEAD + n + 1]]

        def advance(at):
            queue[at - AHEAD][0].wait_send()
            send, n = queue[at]
            if n is not None:
                part = outer_a.at[blocks, pieces[n], :]
                to_row(part, part, a_send.at[NCH + n], a_recv.at[n], outer).wait_recv()
            send.start()

        sends = [to_row(own_tab, inner_tab, tab_send.at[0], tab_recv.at[1], inner)]
        for n, target in enumerate(others()):
            sends.append(
                to_col(own_tab, own_bt.at[col], bt_send.at[0, n], bt_recv.at[0, col], target)
            )
            sends.append(
                to_col(b_ref.at[0, 0, 0], own_b.at[col], b_send.at[0, n], b_recv.at[0, col], target)
            )
        for send in sends[:1] + mine[:AHEAD] + sends[1:]:
            send.start()

        def passed_b():
            out = []
            for n, target in enumerate(others()):
                out.append(
                    to_col(outer_bt.at[col], outer_bt.at[col], bt_send.at[1, n], bt_recv.at[1, col], target)
                )
                out.append(
                    to_col(outer_b.at[col], outer_b.at[col], b_send.at[1, n], b_recv.at[1, col], target)
                )
            return out

        to_row(outer_tab, outer_tab, tab_send.at[1], tab_recv.at[0], outer).wait_recv()
        onward = [to_row(outer_tab, far_tab, tab_send.at[1], tab_recv.at[2], inner)]
        onward[0].start()
        to_row(outer_bt.at[col], outer_bt.at[col], tab_send.at[1], bt_recv.at[1, col], outer).wait_recv()
        to_row(outer_b.at[col], outer_b.at[col], tab_send.at[1], b_recv.at[1, col], outer).wait_recv()

        @pl.when(col != outer)
        def _():
            for send in passed_b():
                send.start()

        for at in range(AHEAD, EARLY):
            advance(at)

        for source in others():
            to_col(own_bt.at[source], own_bt.at[source], bt_send.at[0, 0], bt_recv.at[0, source], col).wait_recv()
            to_col(own_b.at[source], own_b.at[source], b_send.at[0, 0], b_recv.at[0, source], col).wait_recv()

            @pl.when(source != outer)
            def _():
                to_col(outer_bt.at[source], outer_bt.at[source], bt_send.at[0, 0], bt_recv.at[1, source], col).wait_recv()
                to_col(outer_b.at[source], outer_b.at[source], b_send.at[0, 0], b_recv.at[1, source], col).wait_recv()

        to_row(inner_tab, inner_tab, tab_send.at[1], tab_recv.at[1], inner).wait_recv()
        to_row(far_tab, far_tab, tab_send.at[1], tab_recv.at[2], inner).wait_recv()
        loads = [
            to_smem(src, dst, n)
            for n, (src, dst) in enumerate(
                (
                    (own_tab, own_st), (inner_tab, inner_st), (outer_tab, outer_st),
                    (far_tab, far_st), (own_bt, own_bs), (outer_bt, outer_bs),
                )
            )
        ]
        for load in loads:
            load.start()
        copy_a.wait()
        copy_b.wait()
        for load in loads:
            load.wait()
        tabs = (own_st, inner_st, far_st, outer_st)
        own_slots = [looked_up(tab, own_bs, panel) for tab, panel in zip(tabs, panels)]
        outer_slots = [looked_up(tab, outer_bs, panel) for tab, panel in zip(tabs[:3], panels)]
        for at in range(3):
            place_b(outer_w, at, outer_b, outer_bs, panels[at])
        outer_sum[...] = times(picked(own_a, outer_slots[0]), outer_w, 0)

        def from_inner(n, slots, w_ref):
            x = jnp.concatenate([picked(inner_a[n], slots[1]), picked(far_a[n], slots[2])], axis=1)
            return times(x, w_ref, 1, 2)

        def finish(n):
            total = own_sum[:, pieces[n], :] + from_inner(n, own_slots, own_w)
            for r in range(MR):
                store(r, STARTS[n], CHUNKS[n], total[r])

        at = EARLY
        for n in range(NCH):
            if at < len(queue):
                advance(at)
                at += 1
            to_row(
                inner_a[n].at[blocks], inner_a[n].at[blocks], a_send.at[0], a_recv.at[NCH + n], inner
            ).wait_recv()
            to_row(
                far_a[n].at[blocks], far_a[n].at[blocks], a_send.at[0], a_recv.at[2 * NCH + n], inner
            ).wait_recv()
            outer_sum[:, pieces[n], :] += from_inner(n, outer_slots, outer_w)
            send = to_row(
                outer_sum.at[:, pieces[n], :], sum_in.at[:, pieces[n], :],
                sum_send.at[n], sum_recv.at[n], outer,
            )
            send.start()
            onward.append(send)
            if n == 0:
                for at_w, panel in enumerate(panels):
                    place_b(own_w, at_w, own_b, own_bs, panel)
                own_sum[...] = times(picked(own_a, own_slots[0]), own_w, 0)
            if n == NCH - 2:
                own_sum[...] += times(picked(outer_a, own_slots[3]), own_w, 3)
                for done in range(NCH - 2):
                    finish(done)
        finish(NCH - 2)
        finish(NCH - 1)
        for send in sends + onward + [entry[0] for entry in queue[-AHEAD:]]:
            send.wait_send()

        @pl.when(col != outer)
        def _():
            for send in passed_b():
                send.wait_send()


def line_local(a_blocks, a_index, a_live, b_blocks, b_index, c_keep):
    anywhere = pl.BlockSpec(memory_space=pltpu.HBM)
    dma = pltpu.SemaphoreType.DMA
    panel = pltpu.VMEM((NZA + 1, BS, BS), jnp.bfloat16)
    meta = (1, BS)
    total = pltpu.VMEM((MR, BS, WIDE), jnp.float32)
    return pl.pallas_call(
        line_kernel,
        out_shape=pltpu.VMEM((MR * BS, WIDE), jnp.bfloat16),
        in_specs=[anywhere] * 6,
        out_specs=pl.BlockSpec(memory_space=pltpu.VMEM),
        scratch_shapes=[panel] * 2
        + [[pltpu.VMEM((NZA + 1, size, BS), jnp.bfloat16) for size in CHUNKS]] * 2
        + [pltpu.VMEM((4, NZB, BS, BS), jnp.bfloat16)] * 2
        + [pltpu.VMEM((4 * DEPTH, WIDE), jnp.bfloat16), pltpu.VMEM((3 * DEPTH, WIDE), jnp.bfloat16)]
        + [total] * 3
        + [pltpu.VMEM(meta, jnp.int32)] * 4
        + [pltpu.VMEM((4,) + meta, jnp.int32)] * 2
        + [pltpu.SMEM(meta, jnp.int32)] * 4
        + [pltpu.SMEM((4,) + meta, jnp.int32)] * 2
        + [
            dma((2,)), dma((6,)),
            dma((2 * NCH,)), dma((3 * NCH,)), dma((2,)), dma((3,)),
            dma((2, 3)), dma((2, 4)), dma((2, 3)), dma((2, 4)),
            dma((NCH,)), dma((NCH,)),
        ]
        + [pltpu.SMEM(one.shape, jnp.int32) for one in (a_index, a_live, b_index, c_keep.T)]
        + [dma((4,))],
        compiler_params=pltpu.CompilerParams(
            collective_id=0, has_side_effects=True, vmem_limit_bytes=60 * 1024 * 1024
        ),
    )(a_index, a_live, b_index, c_keep.T, a_blocks, b_blocks)


def solution(mesh):
    placed = (
        P(("groups", "row"), "col", None, None, None),
        P(("groups", "row"), "col", None, None),
        P(("groups", "row"), "col"),
        P(("groups", "row"), "col", None, None, None, None),
        P(("groups", "row"), "col", None, None, None),
        P(("groups", "col"), "row"),
    )
    short_line = mesh.shape["row"] == 4 and mesh.shape["col"] == 4
    return jax.shard_map(
        line_local if short_line else local, mesh=mesh, in_specs=placed, out_specs=P(("groups", "col"), "row"), check_vma=False
    )
```
